32 devices in a mesh: fsdp: 4 (over y, x), tp: 4 (over z), tower: 2 (over core).
Axes of the slice: x: 2, y: 2, z: 4, core: 2. Of those that a mesh axis runs over, the one named last changes fastest.
Arguments:
- images: bfloat16 [4096, 5120], P(('fsdp', 'tower')), may hold values from -61 to 61
- img_weight: bfloat16 [5120, 1024], P('fsdp', 'tp')
- texts: bfloat16 [4096, 1024], P(('fsdp', 'tp', 'tower')), may hold values from -1 to 1
- pair_perm: int32 [4096], P(('fsdp', 'tower')), may hold values from 0 to 4095, as said below
- forget: int32 [4096], P(('fsdp', 'tower')), may hold values 0 or 1
Outputs:
- pair_loss: float32 [4096], P(('fsdp', 'tower'))
- weight_grad: float32 [5120, 1024], P('fsdp', 'tp')
The draws below stay inside these ranges and needn't reach their ends.
Inputs may be any that keep to these rules, and one draw needn't show every extreme that they name: `pair_perm`: each number 0 to 4095 appears once.
All inputs are finite; a program needn't handle non-finite values. No bound on the sum of `forget` on one device may be relied on, other than what follows from the above.
Results may differ from the reference program's by a relative error of at most 0.0036.
Values may be sent and summed in bfloat16 or wider, within the bound.
A program may use at most 64 MiB of HBM per device.

```python
import math
import jax
import jax.numpy as jnp
from jax import lax

IMAGE_WIDTH = 5120
EMBED = 1024
PAIRS = 4096


def base_images(key):
    images = jnp.clip(jax.random.normal(jax.random.fold_in(key, 11), (PAIRS, IMAGE_WIDTH), jnp.float32), -6.0, 6.0)
    return images.astype(jnp.bfloat16)


def base_weight(key):
    weight = jnp.clip(jax.random.normal(jax.random.fold_in(key, 13), (IMAGE_WIDTH, EMBED), jnp.float32), -5.0, 5.0)
    weight = weight * IMAGE_WIDTH ** (-0.5)
    return weight.astype(jnp.bfloat16)


def base_perm(key):
    return jax.random.permutation(jax.random.fold_in(key, 14), PAIRS).astype(jnp.int32)


def draw_images(key, part):
    return base_images(key)


def draw_img_weight(key, part):
    return base_weight(key)


def draw_pair_perm(key, part):
    return base_perm(key)


def draw_texts(key, part):
    texts = jax.random.normal(jax.random.fold_in(key, 15), (PAIRS, EMBED), jnp.float32) * EMBED ** (-0.5)
    texts = jnp.clip(texts, -0.25, 0.25)
    return jnp.clip(texts, -1.0, 1.0).astype(jnp.bfloat16)


def place_ends(values, rng, least, high):
    extent = values.shape
    place = [jax.random.randint(jax.random.fold_in(rng, axis), (), 0, extent[axis]) for axis in range(len(extent))]
    values = values.at[tuple(place)].set(least)
    longest = extent.index(max(extent))
    place[longest] = (place[longest] + 1) % extent[longest]
    return values.at[tuple(place)].set(high)


def setup_inputs(seed: int = 0) -> dict:
    key_list = jax.random.split(jax.random.key(seed), 6)
    images = draw_images(jax.random.fold_in(key_list[5], 71), 0)
    img_weight = draw_img_weight(jax.random.fold_in(key_list[5], 71), 0)
    texts = draw_texts(jax.random.fold_in(key_list[5], 71), 0)
    pair_perm = draw_pair_perm(jax.random.fold_in(key_list[5], 71), 0)
    forget = place_ends((jax.random.randint(key_list[4], (PAIRS,), 0, 4) < 1).astype(jnp.int32), jax.random.fold_in(key_list[4], 1), 0, 1)
    return dict(images=images, img_weight=img_weight, texts=texts, pair_perm=pair_perm, forget=forget)


epsilon = 1e-06
score_scale = 100.0

def reference(images, img_weight, texts, pair_perm, forget):
    emb = jnp.dot(images, img_weight, preferred_element_type=jnp.float32).astype(jnp.bfloat16)
    efloat = emb.astype(jnp.float32)
    rnorm = lax.rsqrt(lax.optimization_barrier(jnp.sum(efloat * efloat, axis=1, keepdims=True)) + epsilon)
    unit = efloat * rnorm
    unit_b = unit.astype(jnp.bfloat16)
    signs = 1.0 - 2.0 * forget.astype(jnp.float32)
    block = math.gcd(PAIRS, 512)
    nblocks = PAIRS // block
    columns = jnp.arange(PAIRS, dtype=jnp.int32)

    def one_block(args):
        unit_rows, perm_rows, sign_rows = args
        logits = score_scale * lax.dot_general(unit_rows, texts, (((1,), (1,)), ((), ())), preferred_element_type=jnp.float32)
        top = lax.optimization_barrier(jnp.max(logits, axis=1, keepdims=True))
        lse = top + jnp.log(lax.optimization_barrier(jnp.sum(jnp.exp(logits - top), axis=1, keepdims=True)))
        hit = perm_rows[:, None] == columns[None, :]
        positive = lax.optimization_barrier(jnp.sum(jnp.where(hit, logits, 0.0), axis=1))
        loss = lse[:, 0] - positive
        weights = (sign_rows[:, None] * (jnp.exp(logits - lse) - hit.astype(jnp.float32))).astype(jnp.bfloat16)
        grad_unit = score_scale * jnp.dot(weights, texts, preferred_element_type=jnp.float32)
        return (loss, grad_unit)
    loss, grad_unit = lax.map(one_block, (unit_b.reshape(nblocks, block, EMBED), pair_perm.reshape(nblocks, block), signs.reshape(nblocks, block)))
    loss = loss.reshape(PAIRS)
    grad_unit = grad_unit.reshape(PAIRS, EMBED)
    radial = lax.optimization_barrier(jnp.sum(unit * grad_unit, axis=1, keepdims=True))
    grad_emb = (rnorm * (grad_unit - unit * radial)).astype(jnp.bfloat16)
    weight_grad = lax.dot_general(images, grad_emb, (((0,), (0,)), ((), ())), preferred_element_type=jnp.float32)
    return (loss, weight_grad)
```

```python
import functools

import jax
import jax.numpy as jnp
from jax import lax
from jax.experimental import pallas as pl
from jax.experimental.pallas import tpu as pltpu
from jax.sharding import PartitionSpec as P

epsilon = 1e-06
score_scale = 100.0
F32 = jnp.float32
BF16 = jnp.bfloat16
NT = (((1,), (1,)), ((), ()))


def spread(columns, lanes):
    n = columns[0].shape[1]
    which = lax.broadcasted_iota(jnp.int32, (lanes, n), 0)
    block = jnp.broadcast_to(columns[0], (lanes, n))
    for k in range(1, len(columns)):
        block = jnp.where(which == k, columns[k], block)
    block = block.T
    return [block[:, k : k + 1] for k in range(len(columns))]


def kernel(sizes, images, weight, texts, perm, forget, loss, out, *scratch):
    F, T, C, R = sizes
    (img, img_t, wall, tall, acc, ebuf, ubuf, lbuf, pbuf, sbuf, gown, gsend, grecv, gemb,
     share, sib_send, sib_recv, wsend, wrecv, obuf,
     loc, w_s, w_r, wf_s, wf_r, t_s, t_r, tf_s, tf_r, to_s, to_r, e_s, e_r, st_s, st_r,
     g_s, g_r, b_s, b_r, x_s, x_r, o_s, o_r) = scratch
    f, t, c = lax.axis_index("fsdp"), lax.axis_index("tp"), lax.axis_index("tower")
    pairs, width = img.shape
    kb, cols = weight.shape
    kh = kb // C
    tr, embed = texts.shape
    bw = tr * C
    rows = pairs // R
    sends = []

    def other(me, d, n):
        return lax.rem(me + d, n)

    def remote(src, dst, ssem, rsem, axis, target):
        return pltpu.make_async_remote_copy(
            src_ref=src, dst_ref=dst, send_sem=ssem, recv_sem=rsem,
            device_id={axis: target}, device_id_type=pl.DeviceIdType.MESH,
        )

    def send(*args):
        copy = remote(*args)
        copy.start()
        sends.append(copy)

    def arrived(dst, ssem, rsem, axis, target):
        remote(dst, dst, ssem, rsem, axis, target).wait_recv()

    def wpart(ff, cc):
        return wall.at[pl.ds(pl.multiple_of(ff * kb + cc * kh, 16), kh)]

    def tpart(ff, cc):
        return tall.at[ff, pl.ds(pl.multiple_of(cc * tr, 16), tr)]

    img_copy = pltpu.make_async_copy(images, img, loc.at[0])
    img_copy.start()
    w_copy = pltpu.make_async_copy(
        weight, wall.at[pl.ds(pl.multiple_of(f * kb, 16), kb)], loc.at[1])
    w_copy.start()
    t_copy = pltpu.make_async_copy(texts, tpart(f, c), loc.at[2])
    t_copy.start()

    barrier = pltpu.get_barrier_semaphore()
    for axis, me, n in (("fsdp", f, F), ("tp", t, T), ("tower", c, C)):
        for d in range(1, n):
            pl.semaphore_signal(barrier, inc=1, device_id={axis: other(me, d, n)},
                                device_id_type=pl.DeviceIdType.MESH)
    pl.semaphore_wait(barrier, F + T + C - 3)

    mine = weight.at[pl.ds(pl.multiple_of(c * kh, 16), kh)]
    for d in range(1, F):
        send(mine, wpart(f, c), w_s.at[d], w_r.at[d], "fsdp", other(f, d, F))
    for d in range(1, F):
        send(texts, tpart(f, c), t_s.at[d], t_r.at[d], "fsdp", other(f, d, F))
    for e in range(1, C):
        send(texts, tpart(f, c), to_s.at[e], to_r.at[e], "tower", other(c, e, C))

    img_copy.wait()
    w_copy.wait()
    aligned = kb % 128 == 0

    def by_k(ff):
        k = pl.multiple_of(ff * kb, kb)
        return jnp.dot(img[:, pl.ds(k, kb)], wall[pl.ds(k, kb), :], preferred_element_type=F32)

    if aligned:
        acc[...] = by_k(f)

    def turn(k, carry):
        k = pl.multiple_of(k * 128, 128)
        img_t[pl.ds(k, 128), :] = img[:, pl.ds(k, 128)].T
        return carry

    lax.fori_loop(0, width // 128, turn, 0)

    def w_from(d):
        ff = other(f, F - d, F)
        arrived(wpart(ff, c), w_s.at[d], w_r.at[d], "fsdp", ff)
        for e in range(1, C):
            send(wpart(ff, c), wpart(ff, c), wf_s.at[d, e], wf_r.at[d, e], "tower", other(c, e, C))

    def w_rest(d):
        ff = other(f, F - d, F)
        for e in range(1, C):
            cc = other(c, C - e, C)
            arrived(wpart(ff, cc), wf_s.at[d, e], wf_r.at[d, e], "tower", cc)
        if aligned:
            acc[...] += by_k(ff)

    for d in range(1, F):
        w_from(d)
        if d > 1:
            w_rest(d - 1)
    w_rest(F - 1)
    if not aligned:
        acc[...] = jnp.zeros_like(acc)

        def by_tile(k, carry):
            k = pl.multiple_of(k * 128, 128)
            acc[...] += jnp.dot(img[:, pl.ds(k, 128)], wall[pl.ds(k, 128), :],
                                preferred_element_type=F32)
            return carry

        lax.fori_loop(0, width // 128, by_tile, 0)

    for r in range(R):
        ebuf[r, t] = acc[r * rows : (r + 1) * rows, :].astype(BF16)
        for d in range(1, T):
            send(ebuf.at[r, t], ebuf.at[r, t], e_s.at[r, d], e_r.at[r, d], "tp", other(t, d, T))

    t_copy.wait()
    for d in range(1, F):
        ff = other(f, F - d, F)
        arrived(tpart(ff, c), t_s.at[d], t_r.at[d], "fsdp", ff)
        for e in range(1, C):
            send(tpart(ff, c), tpart(ff, c), tf_s.at[d, e], tf_r.at[d, e], "tower", other(c, e, C))
    for e in range(1, C):
        cc = other(c, C - e, C)
        arrived(tpart(f, cc), to_s.at[e], to_r.at[e], "tower", cc)
    for d in range(1, F):
        ff = other(f, F - d, F)
        for e in range(1, C):
            cc = other(c, C - e, C)
            arrived(tpart(ff, cc), tf_s.at[d, e], tf_r.at[d, e], "tower", cc)

    kept = []
    for r in range(R):
        for d in range(1, T):
            tt = other(t, T - d, T)
            arrived(ebuf.at[r, tt], e_s.at[r, d], e_r.at[r, d], "tp", tt)
        square = jnp.zeros((rows, 1), F32)
        for k in range(T):
            part = ebuf[r, k].astype(F32)
            square += jnp.sum(part * part, axis=1, keepdims=True)
        rnorm = lax.rsqrt(square + epsilon)
        for k in range(T):
            ubuf[:, k * cols : (k + 1) * cols] = (ebuf[r, k].astype(F32) * rnorm).astype(BF16)

        span = slice(r * rows, (r + 1) * rows)
        sign_row = 1.0 - 2.0 * forget[:, span].astype(F32)
        permf, = spread([perm[:, span].astype(F32)], 128)
        lane = lax.broadcasted_iota(jnp.int32, (1, bw), 1)

        def hits(j):
            return permf == ((j * T + t) * bw + lane).astype(F32)

        def score(j, top):
            logit = score_scale * lax.dot_general(ubuf[...], tall[j], NT, preferred_element_type=F32)
            lbuf[j] = logit
            return jnp.maximum(top, jnp.max(logit, axis=1, keepdims=True))

        top = lax.fori_loop(0, F, score, jnp.full((rows, 1), -jnp.inf, F32))

        def totals(j, so_far):
            total, first, positive = so_far
            logit = lbuf[j]
            power = jnp.exp(logit - top)
            return (
                total + jnp.sum(power, axis=1, keepdims=True),
                first + jnp.sum(power * logit, axis=1, keepdims=True),
                positive + jnp.sum(jnp.where(hits(j), logit, 0.0), axis=1, keepdims=True),
            )

        zero = jnp.zeros((rows, 1), F32)
        total, first, positive = lax.fori_loop(0, F, totals, (zero, zero, zero))
        place = lax.broadcasted_iota(jnp.int32, (rows, 128), 1)
        packed = jnp.where(place == 0, top, jnp.where(place == 1, total,
                           jnp.where(place == 2, first, positive)))
        sbuf[r, t] = packed.T[:8]
        for d in range(1, T):
            send(sbuf.at[r, t], sbuf.at[r, t], st_s.at[r, d], st_r.at[r, d], "tp", other(t, d, T))
        for d in range(1, T):
            tt = other(t, T - d, T)
            arrived(sbuf.at[r, tt], st_s.at[r, d], st_r.at[r, d], "tp", tt)
        peak = sbuf[r, 0, 0:1, :]
        for k in range(1, T):
            peak = jnp.maximum(peak, sbuf[r, k, 0:1, :])
        total = jnp.zeros_like(peak)
        first = jnp.zeros_like(peak)
        positive = jnp.zeros_like(peak)
        for k in range(T):
            scale = jnp.exp(sbuf[r, k, 0:1, :] - peak)
            total += scale * sbuf[r, k, 1:2, :]
            first += scale * sbuf[r, k, 2:3, :]
            positive += sbuf[r, k, 3:4, :]
        lse_row = peak + jnp.log(total)
        loss[:, span] = lse_row - positive
        lse, sign, radial = spread([lse_row, sign_row, sign_row * (first / total - positive)], 128)

        def weigh(j, carry):
            pbuf[j] = (sign * (jnp.exp(lbuf[j] - lse) - hits(j).astype(F32))).astype(BF16)
            return carry

        lax.fori_loop(0, F, weigh, 0)

        def grad_for(tt):
            place = pl.ds(pl.multiple_of(tt * cols, cols), cols)
            total = jnp.dot(pbuf[0], tall[0, :, place], preferred_element_type=F32)
            for j in range(1, F):
                total += jnp.dot(pbuf[j], tall[j, :, place], preferred_element_type=F32)
            return score_scale * total

        for d in range(1, T):
            tt = other(t, d, T)
            gsend[r, d] = grad_for(tt).astype(BF16)
            send(gsend.at[r, d], grecv.at[r, d], g_s.at[r, d], g_r.at[r, d], "tp", tt)
        gown[r] = grad_for(t)
        kept.append((rnorm, radial))

    for r in range(R):
        rnorm, radial = kept[r]
        grad = gown[r]
        for d in range(1, T):
            arrived(grecv.at[r, d], g_s.at[r, d], g_r.at[r, d], "tp", other(t, T - d, T))
            grad += grecv[r, d].astype(F32)
        unit = ebuf[r, t].astype(F32) * rnorm
        gemb[r * rows : (r + 1) * rows, :] = (rnorm * (grad - unit * radial)).astype(BF16)

    def block(ff, cc):
        k = pl.multiple_of(ff * kb + cc * kh, 16)
        return jnp.dot(img_t[pl.ds(k, kh), :], gemb[...], preferred_element_type=F32)

    def compute(d):
        ff = other(f, d, F)
        for e in range(1, C):
            cc = other(c, e, C)
            sib_send[d, e] = block(ff, cc)
            send(sib_send.at[d, e], sib_recv.at[d, e], b_s.at[d, e], b_r.at[d, e], "tower", cc)
        share[d] = block(ff, c)

    def joined(d):
        total = share[d]
        for e in range(1, C):
            arrived(sib_recv.at[d, e], b_s.at[d, e], b_r.at[d, e], "tower", other(c, C - e, C))
            total += sib_recv[d, e]
        return total

    def dispatch(d):
        wsend[d] = joined(d).astype(BF16)
        send(wsend.at[d], wrecv.at[d], x_s.at[d], x_r.at[d], "fsdp", other(f, d, F))

    for d in range(1, F):
        compute(d)
        if d > 1:
            dispatch(d - 1)
    compute(0)
    dispatch(F - 1)
    total = joined(0)
    for d in range(1, F):
        arrived(wrecv.at[d], x_s.at[d], x_r.at[d], "fsdp", other(f, F - d, F))
        total += wrecv[d].astype(F32)
    obuf[c] = total
    for e in range(1, C):
        send(obuf.at[c], obuf.at[c], o_s.at[e], o_r.at[e], "tower", other(c, e, C))
    home = pltpu.make_async_copy(obuf.at[c], out.at[c], loc.at[3])
    home.start()
    for e in range(1, C):
        cc = other(c, C - e, C)
        arrived(obuf.at[cc], o_s.at[e], o_r.at[e], "tower", cc)
        away = pltpu.make_async_copy(obuf.at[cc], out.at[cc], loc.at[3 + e])
        away.start()
        away.wait()
    home.wait()
    for copy in sends:
        copy.wait_send()


def local(images, weight, texts, perm, forget):
    F, T, C = lax.axis_size("fsdp"), lax.axis_size("tp"), lax.axis_size("tower")
    R = 2
    pairs, width = images.shape
    kb, cols = weight.shape
    kh = kb // C
    tr, embed = texts.shape
    rows = pairs // R
    bw = tr * C
    vmem, dma = pltpu.VMEM, pltpu.SemaphoreType.DMA
    scratch = [
        vmem((pairs, width), BF16),
        vmem((width, pairs), BF16),
        vmem((width, cols), BF16),
        vmem((F, bw, embed), BF16),
        vmem((pairs, cols), F32),
        vmem((R, T, rows, cols), BF16),
        vmem((rows, embed), BF16),
        vmem((F, rows, bw), F32),
        vmem((F, rows, bw), BF16),
        vmem((R, T, 8, rows), F32),
        vmem((R, rows, cols), F32),
        vmem((R, T, rows, cols), BF16),
        vmem((R, T, rows, cols), BF16),
        vmem((pairs, cols), BF16),
        vmem((F, kh, cols), F32),
        vmem((F, C, kh, cols), F32),
        vmem((F, C, kh, cols), F32),
        vmem((F, kh, cols), BF16),
        vmem((F, kh, cols), BF16),
        vmem((C, kh, cols), F32),
        dma((3 + C,)),
        dma((F,)), dma((F,)), dma((F, C)), dma((F, C)),
        dma((F,)), dma((F,)), dma((F, C)), dma((F, C)),
        dma((C,)), dma((C,)),
        dma((R, T)), dma((R, T)), dma((R, T)), dma((R, T)),
        dma((R, T)), dma((R, T)),
        dma((F, C)), dma((F, C)), dma((F,)), dma((F,)),
        dma((C,)), dma((C,)),
    ]
    any_space = pl.BlockSpec(memory_space=pl.ANY)
    whole = pl.BlockSpec(memory_space=pltpu.VMEM)
    loss, out = pl.pallas_call(
        functools.partial(kernel, (F, T, C, R)),
        out_shape=(
            jax.ShapeDtypeStruct((1, pairs), F32),
            jax.ShapeDtypeStruct((C, kh, cols), F32),
        ),
        in_specs=[any_space, any_space, any_space, whole, whole],
        out_specs=(whole, any_space),
        scratch_shapes=scratch,
        compiler_params=pltpu.CompilerParams(
            collective_id=0, has_side_effects=True, vmem_limit_bytes=56 * 2**20
        ),
        cost_estimate=pl.CostEstimate(
            flops=4 * pairs * cols * width + 4 * pairs * F * bw * embed,
            bytes_accessed=2 * (pairs * width + kb * cols + tr * embed) + 4 * kb * cols,
            transcendentals=2 * pairs * F * bw,
        ),
    )(images, weight, texts, perm.reshape(1, pairs), forget.reshape(1, pairs))
    return loss.reshape(pairs), out.reshape(kb, cols)


def solution(mesh):
    return jax.shard_map(
        local,
        mesh=mesh,
        in_specs=(
            P(("fsdp", "tower"), None),
            P("fsdp", "tp"),
            P(("fsdp", "tp", "tower"), None),
            P(("fsdp", "tower")),
            P(("fsdp", "tower")),
        ),
        out_specs=(P(("fsdp", "tower")), P("fsdp", "tp")),
        check_vma=False,
    )
```

```python
import functools

import jax
import jax.numpy as jnp
from jax import lax
from jax.experimental import pallas as pl
from jax.experimental.pallas import tpu as pltpu
from jax.sharding import PartitionSpec as P

epsilon = 1e-06
score_scale = 100.0
F32 = jnp.float32
BF16 = jnp.bfloat16
NT = (((1,), (1,)), ((), ()))


def spread(columns, lanes):
    n = columns[0].shape[1]
    which = lax.broadcasted_iota(jnp.int32, (lanes, n), 0)
    block = jnp.broadcast_to(columns[0], (lanes, n))
    for k in range(1, len(columns)):
        block = jnp.where(which == k, columns[k], block)
    block = block.T
    return [block[:, k : k + 1] for k in range(len(columns))]


def kernel(sizes, images, weight, texts, perm, forget, loss, out, *scratch):
    F, T, C = sizes
    (img, img_t, wall, tall, acc, eown, ebuf, ubuf, lbuf, pbuf, sbuf, gown, gsend, grecv, gemb,
     share, sib_send, sib_recv, wsend, wrecv, obuf,
     loc, w_s, w_r, wf_s, wf_r, t_s, t_r, tf_s, tf_r, to_s, to_r, tp_s, tp_r, e_s, e_r, st_s, st_r,
     g_s, g_r, b_s, b_r, x_s, x_r, o_s, o_r) = scratch
    f, t, c = lax.axis_index("fsdp"), lax.axis_index("tp"), lax.axis_index("tower")
    q, h = lax.div(t, 2), lax.rem(t, 2)
    pairs, width = img.shape
    half = pairs // 2
    kb, cols = weight.shape
    kh = kb // C
    tr, embed = texts.shape
    bw = 2 * tr * C
    square_plane = F == 4
    sends = []

    def other(me, d, n):
        return lax.rem(me + d, n)

    def fsdp_to(d):
        if not square_plane:
            return lax.rem(f + d, F)
        high, low = lax.div(f, 2), lax.rem(f, 2)
        return 2 * (1 - high if d & 2 else high) + (1 - low if d & 1 else low)

    def fsdp_from(d):
        return fsdp_to(d) if square_plane else lax.rem(f + F - d, F)

    def remote(src, dst, ssem, rsem, axis, target):
        return pltpu.make_async_remote_copy(
            src_ref=src, dst_ref=dst, send_sem=ssem, recv_sem=rsem,
            device_id={axis: target}, device_id_type=pl.DeviceIdType.MESH,
        )

    def send(*args):
        copy = remote(*args)
        copy.start()
        sends.append(copy)

    def arrived(dst, ssem, rsem, axis, target):
        remote(dst, dst, ssem, rsem, axis, target).wait_recv()

    def gather_start(mine, part, size, ssem, rsem):
        for d in (1, 2) if square_plane else range(1, F):
            send(mine, part(f, 0, size), ssem(d), rsem(d), "fsdp", fsdp_to(d))

    def gather_wait(d, part, size, ssem, rsem):
        ff = fsdp_from(d)
        if not square_plane:
            arrived(part(ff, 0, size), ssem(d), rsem(d), "fsdp", ff)
        elif d < 3:
            arrived(part(ff, 0, size), ssem(d), rsem(d), "fsdp", ff)
            piece = part(ff, (d - 1) * (size // 2), size // 2)
            send(piece, piece, ssem(2 + d), rsem(2 + d), "fsdp", fsdp_to(3 - d))
        else:
            for k in (0, 1):
                arrived(part(ff, k * (size // 2), size // 2), ssem(3 + k), rsem(3 + k),
                        "fsdp", fsdp_from(2 - k))

    def share_out(block, ssem, rsem):
        for e in range(1, C):
            send(block, block, ssem(e), rsem(e), "tower", other(c, e, C))

    def shared_in(block, ssem, rsem):
        for e in range(1, C):
            cc = other(c, C - e, C)
            arrived(block(cc), ssem(e), rsem(e), "tower", cc)

    def wpart(cc):
        return lambda ff, lo, n: wall.at[pl.ds(pl.multiple_of(ff * kb + cc * kh + lo, 16), n)]

    def tpart(p, cc):
        return lambda ff, lo, n: tall.at[ff, pl.ds(pl.multiple_of((p * C + cc) * tr + lo, 16), n)]

    img_copy = pltpu.make_async_copy(images, img, loc.at[0])
    img_copy.start()
    w_copy = pltpu.make_async_copy(
        weight, wall.at[pl.ds(pl.multiple_of(f * kb, 16), kb)], loc.at[1])
    w_copy.start()
    t_copy = pltpu.make_async_copy(texts, tpart(h, c)(f, 0, tr), loc.at[2])
    t_copy.start()

    barrier = pltpu.get_barrier_semaphore()
    for axis, me, n in (("fsdp", f, F), ("tp", t, T), ("tower", c, C)):
        for d in range(1, n):
            pl.semaphore_signal(barrier, inc=1, device_id={axis: other(me, d, n)},
                                device_id_type=pl.DeviceIdType.MESH)
    pl.semaphore_wait(barrier, F + T + C - 3)

    w_sems = (lambda d: w_s.at[d]), (lambda d: w_r.at[d])
    gather_start(weight.at[pl.ds(pl.multiple_of(c * kh, 16), kh)], wpart(c), kh, *w_sems)
    partner = 2 * q + 1 - h
    send(texts, tpart(h, c)(f, 0, tr), tp_s.at[0], tp_r.at[0], "tp", partner)
    for e in range(1, C):
        send(texts, tpart(h, c)(f, 0, tr), to_s.at[0, e], to_r.at[0, e], "tower", other(c, e, C))

    img_copy.wait()
    w_copy.wait()
    aligned = kb % 128 == 0

    def by_k(ff):
        k = pl.multiple_of(ff * kb, kb)
        return jnp.dot(img[:, pl.ds(k, kb)], wall[pl.ds(k, kb), :], preferred_element_type=F32)

    if aligned:
        acc[...] = by_k(f)

    def turn(k, carry):
        k = pl.multiple_of(k * 128, 128)
        img_t[pl.ds(k, 128), :] = img[:, pl.ds(k, 128)].T
        return carry

    lax.fori_loop(0, width // 128, turn, 0)

    def wf(d):
        return (lambda e: wf_s.at[d, e]), (lambda e: wf_r.at[d, e])

    def w_from(d):
        gather_wait(d, wpart(c), kh, *w_sems)
        share_out(wpart(c)(fsdp_from(d), 0, kh), *wf(d))

    def w_rest(d):
        ff = fsdp_from(d)
        shared_in(lambda cc: wpart(cc)(ff, 0, kh), *wf(d))
        if aligned:
            acc[...] += by_k(ff)

    def t_sems(k):
        return (lambda d: t_s.at[k, d]), (lambda d: t_r.at[k, d])

    def tf(k, d):
        return (lambda e: tf_s.at[k, d, e]), (lambda e: tf_r.at[k, d, e])

    def to(k):
        return (lambda e: to_s.at[k, e]), (lambda e: to_r.at[k, e])

    sides = (h, 1 - h)
    for d in range(1, F - 1):
        w_from(d)
    gather_start(texts, tpart(h, c), tr, *t_sems(0))
    for d in range(1, F - 1):
        w_rest(d)
    theirs = tpart(1 - h, c)(f, 0, tr)
    arrived(theirs, tp_s.at[0], tp_r.at[0], "tp", partner)
    share_out(theirs, *to(1))
    w_from(F - 1)
    gather_start(theirs, tpart(1 - h, c), tr, *t_sems(1))
    w_rest(F - 1)
    if not aligned:
        acc[...] = jnp.zeros_like(acc)

        def by_tile(k, carry):
            k = pl.multiple_of(k * 128, 128)
            acc[...] += jnp.dot(img[:, pl.ds(k, 128)], wall[pl.ds(k, 128), :],
                                preferred_element_type=F32)
            return carry

        lax.fori_loop(0, width // 128, by_tile, 0)

    for k in range(2):
        eown[k] = acc[k * half : (k + 1) * half, :].astype(BF16)
    for d in range(1, T):
        tt = other(t, d, T)
        send(eown.at[lax.rem(tt, 2)], ebuf.at[t], e_s.at[d], e_r.at[d], "tp", tt)
    ebuf[t] = eown[h]

    def t_from(k, d):
        gather_wait(d, tpart(sides[k], c), tr, *t_sems(k))
        share_out(tpart(sides[k], c)(fsdp_from(d), 0, tr), *tf(k, d))

    def t_rest(k, d):
        ff = fsdp_from(d)
        shared_in(lambda cc: tpart(sides[k], cc)(ff, 0, tr), *tf(k, d))

    t_copy.wait()
    for k in range(2):
        for d in range(1, F - 1):
            t_from(k, d)
    for k in range(2):
        shared_in(lambda cc: tpart(sides[k], cc)(f, 0, tr), *to(k))

    for d in range(1, T):
        tt = other(t, T - d, T)
        arrived(ebuf.at[tt], e_s.at[d], e_r.at[d], "tp", tt)
    square = jnp.zeros((half, 1), F32)
    for k in range(T):
        part = ebuf[k].astype(F32)
        square += jnp.sum(part * part, axis=1, keepdims=True)
    rnorm = lax.rsqrt(square + epsilon)
    for k in range(T):
        ubuf[:, k * cols : (k + 1) * cols] = (ebuf[k].astype(F32) * rnorm).astype(BF16)

    span = pl.ds(pl.multiple_of(h * half, half), half)
    permf, = spread([perm[:, span].astype(F32)], 128)
    lane = lax.broadcasted_iota(jnp.int32, (1, bw), 1)

    def hits(j):
        return permf == ((j * T + 2 * q) * (bw // 2) + lane).astype(F32)

    def score(j, top):
        logit = score_scale * lax.dot_general(ubuf[...], tall[j], NT, preferred_element_type=F32)
        lbuf[j] = logit
        return jnp.maximum(top, jnp.max(logit, axis=1, keepdims=True))

    top = score(f, jnp.full((half, 1), -jnp.inf, F32))
    for d in range(1, F):
        for k in range(2):
            if d == F - 1:
                t_from(k, d)
        for k in range(2):
            t_rest(k, d)
        top = score(fsdp_from(d), top)

    def totals(j, so_far):
        total, first, positive = so_far
        logit = lbuf[j]
        power = jnp.exp(logit - top)
        return (
            total + jnp.sum(power, axis=1, keepdims=True),
            first + jnp.sum(power * logit, axis=1, keepdims=True),
            positive + jnp.sum(jnp.where(hits(j), logit, 0.0), axis=1, keepdims=True),
        )

    zero = jnp.zeros((half, 1), F32)
    total, first, positive = lax.fori_loop(0, F, totals, (zero, zero, zero))
    place = lax.broadcasted_iota(jnp.int32, (half, 128), 1)
    packed = jnp.where(place == 0, top, jnp.where(place == 1, total,
                       jnp.where(place == 2, first, jnp.where(place == 3, positive, rnorm))))
    sbuf[t] = packed.T[:8]
    for d in range(1, T):
        send(sbuf.at[t], sbuf.at[t], st_s.at[d], st_r.at[d], "tp", other(t, d, T))

    def stats_from(d):
        tt = other(t, T - d, T)
        arrived(sbuf.at[tt], st_s.at[d], st_r.at[d], "tp", tt)

    def combined(group):
        peak = sbuf[group, 0:1, :]
        for k in range(1, T // 2):
            peak = jnp.maximum(peak, sbuf[2 * k + group, 0:1, :])
        total = jnp.zeros_like(peak)
        first = jnp.zeros_like(peak)
        positive = jnp.zeros_like(peak)
        for k in range(T // 2):
            scale = jnp.exp(sbuf[2 * k + group, 0:1, :] - peak)
            total += scale * sbuf[2 * k + group, 1:2, :]
            first += scale * sbuf[2 * k + group, 2:3, :]
            positive += sbuf[2 * k + group, 3:4, :]
        return peak + jnp.log(total), first / total, positive

    def sign_of(places):
        return 1.0 - 2.0 * forget[:, places].astype(F32)

    for d in range(2, T, 2):
        stats_from(d)
    lse_row, _, _ = combined(h)
    lse, sign = spread([lse_row, sign_of(span)], 128)

    def weigh(j, carry):
        pbuf[j] = (sign * (jnp.exp(lbuf[j] - lse) - hits(j).astype(F32))).astype(BF16)
        return carry

    lax.fori_loop(0, F, weigh, 0)

    def grad_for(tt):
        place = pl.ds(pl.multiple_of(tt * cols, cols), cols)
        total = jnp.dot(pbuf[0], tall[0, :, place], preferred_element_type=F32)
        for j in range(1, F):
            total += jnp.dot(pbuf[j], tall[j, :, place], preferred_element_type=F32)
        return score_scale * total

    for d in range(1, T):
        tt = other(t, d, T)
        gsend[d] = grad_for(tt).astype(BF16)
        send(gsend.at[d], grecv.at[t], g_s.at[d], g_r.at[d], "tp", tt)
    gown[h] = grad_for(t)
    gown[1 - h] = jnp.zeros((half, cols), F32)
    grecv[t] = jnp.zeros((half, cols), BF16)

    for d in range(1, T, 2):
        stats_from(d)
    kept = []
    for k in range(2):
        places = slice(k * half, (k + 1) * half)
        lse_row, mean_row, positive = combined(k)
        loss[:, places] = lse_row - positive
        kept.append(spread([sign_of(places) * (mean_row - positive), sbuf[k, 4:5, :]], 128))
    for d in range(1, T):
        tt = other(t, T - d, T)
        arrived(grecv.at[tt], g_s.at[d], g_r.at[d], "tp", tt)
    for k in range(2):
        radial, rnorm = kept[k]
        grad = gown[k]
        for j in range(T // 2):
            grad += grecv[2 * j + k].astype(F32)
        unit = eown[k].astype(F32) * rnorm
        gemb[k * half : (k + 1) * half, :] = (rnorm * (grad - unit * radial)).astype(BF16)

    def block(ff, cc):
        k = pl.multiple_of(ff * kb + cc * kh, 16)
        return jnp.dot(img_t[pl.ds(k, kh), :], gemb[...], preferred_element_type=F32)

    def compute(d):
        ff = fsdp_to(d)
        for e in range(1, C):
            cc = other(c, e, C)
            sib_send[d, e] = block(ff, cc)
            send(sib_send.at[d, e], sib_recv.at[d, e], b_s.at[d, e], b_r.at[d, e], "tower", cc)
        share[d] = block(ff, c)

    def joined(d):
        total = share[d]
        for e in range(1, C):
            arrived(sib_recv.at[d, e], b_s.at[d, e], b_r.at[d, e], "tower", other(c, C - e, C))
            total += sib_recv[d, e]
        return total

    def dispatch(d):
        wsend[d] = joined(d).astype(BF16)
        send(wsend.at[d], wrecv.at[d], x_s.at[d], x_r.at[d], "fsdp", fsdp_to(d))

    for d in range(F - 1, 0, -1):
        compute(d)
        if d < F - 1:
            dispatch(d + 1)
    compute(0)
    dispatch(1)
    total = joined(0)
    for d in range(F - 1, 0, -1):
        arrived(wrecv.at[d], x_s.at[d], x_r.at[d], "fsdp", fsdp_from(d))
        total += wrecv[d].astype(F32)
    obuf[c] = total
    share_out(obuf.at[c], lambda e: o_s.at[e], lambda e: o_r.at[e])
    home = pltpu.make_async_copy(obuf.at[c], out.at[c], loc.at[3])
    home.start()
    for e in range(1, C):
        cc = other(c, C - e, C)
        arrived(obuf.at[cc], o_s.at[e], o_r.at[e], "tower", cc)
        away = pltpu.make_async_copy(obuf.at[cc], out.at[cc], loc.at[3 + e])
        away.start()
        away.wait()
    home.wait()
    for copy in sends:
        copy.wait_send()


def local(images, weight, texts, perm, forget):
    F, T, C = lax.axis_size("fsdp"), lax.axis_size("tp"), lax.axis_size("tower")
    assert T % 2 == 0
    pairs, width = images.shape
    kb, cols = weight.shape
    kh = kb // C
    tr, embed = texts.shape
    half = pairs // 2
    bw = 2 * tr * C
    vmem, dma = pltpu.VMEM, pltpu.SemaphoreType.DMA
    scratch = [
        vmem((pairs, width), BF16),
        vmem((width, pairs), BF16),
        vmem((width, cols), BF16),
        vmem((F, bw, embed), BF16),
        vmem((pairs, cols), F32),
        vmem((2, half, cols), BF16),
        vmem((T, half, cols), BF16),
        vmem((half, embed), BF16),
        vmem((F, half, bw), F32),
        vmem((F, half, bw), BF16),
        vmem((T, 8, half), F32),
        vmem((2, half, cols), F32),
        vmem((T, half, cols), BF16),
        vmem((T, half, cols), BF16),
        vmem((pairs, cols), BF16),
        vmem((F, kh, cols), F32),
        vmem((F, C, kh, cols), F32),
        vmem((F, C, kh, cols), F32),
        vmem((F, kh, cols), BF16),
        vmem((F, kh, cols), BF16),
        vmem((C, kh, cols), F32),
        dma((3 + C,)),
        dma((F + 1,)), dma((F + 1,)), dma((F, C)), dma((F, C)),
        dma((2, F + 1)), dma((2, F + 1)), dma((2, F, C)), dma((2, F, C)),
        dma((2, C)), dma((2, C)), dma((1,)), dma((1,)),
        dma((T,)), dma((T,)), dma((T,)), dma((T,)),
        dma((T,)), dma((T,)),
        dma((F, C)), dma((F, C)), dma((F,)), dma((F,)),
        dma((C,)), dma((C,)),
    ]
    any_space = pl.BlockSpec(memory_space=pl.ANY)
    whole = pl.BlockSpec(memory_space=pltpu.VMEM)
    loss, out = pl.pallas_call(
        functools.partial(kernel, (F, T, C)),
        out_shape=(
            jax.ShapeDtypeStruct((1, pairs), F32),
            jax.ShapeDtypeStruct((C, kh, cols), F32),
        ),
        in_specs=[any_space, any_space, any_space, whole, whole],
        out_specs=(whole, any_space),
        scratch_shapes=scratch,
        compiler_params=pltpu.CompilerParams(
            collective_id=0, has_side_effects=True, vmem_limit_bytes=60 * 2**20
        ),
        cost_estimate=pl.CostEstimate(
            flops=4 * pairs * cols * width + 4 * half * F * bw * embed,
            bytes_accessed=2 * (pairs * width + kb * cols + tr * embed) + 4 * kb * cols,
            transcendentals=2 * half * F * bw,
        ),
    )(images, weight, texts, perm.reshape(1, pairs), forget.reshape(1, pairs))
    return loss.reshape(pairs), out.reshape(kb, cols)


def solution(mesh):
    return jax.shard_map(
        local,
        mesh=mesh,
        in_specs=(
            P(("fsdp", "tower"), None),
            P("fsdp", "tp"),
            P(("fsdp", "tp", "tower"), None),
            P(("fsdp", "tower")),
            P(("fsdp", "tower")),
        ),
        out_specs=(P(("fsdp", "tower")), P("fsdp", "tp")),
        check_vma=False,
    )
```

```python
import functools

import jax
import jax.numpy as jnp
from jax import lax
from jax.experimental import pallas as pl
from jax.experimental.pallas import tpu as pltpu
from jax.sharding import PartitionSpec as P

epsilon = 1e-06
score_scale = 100.0
F32 = jnp.float32
BF16 = jnp.bfloat16
NT = (((1,), (1,)), ((), ()))


def spread(columns, lanes):
    n = columns[0].shape[1]
    which = lax.broadcasted_iota(jnp.int32, (lanes, n), 0)
    block = jnp.broadcast_to(columns[0], (lanes, n))
    for k in range(1, len(columns)):
        block = jnp.where(which == k, columns[k], block)
    block = block.T
    return [block[:, k : k + 1] for k in range(len(columns))]


def kernel(sizes, images, weight, texts, perm, forget, loss, out, *scratch):
    F, T, C = sizes
    (img, img_t, wall, tall, acc, eown, ebuf, ubuf, lbuf, pbuf, sbuf, gown, gsend, grecv, gemb,
     share, sib_send, sib_recv, wsend, wrecv, obuf,
     loc, w_s, w_r, wf_s, wf_r, t_s, t_r, tf_s, tf_r, to_s, to_r, tp_s, tp_r, e_s, e_r, st_s, st_r,
     g_s, g_r, b_s, b_r, x_s, x_r, o_s, o_r) = scratch
    f, t, c = lax.axis_index("fsdp"), lax.axis_index("tp"), lax.axis_index("tower")
    q, h = lax.div(t, 2), lax.rem(t, 2)
    pairs, width = img.shape
    half = pairs // 2
    kb, cols = weight.shape
    kh = kb // C
    tr, embed = texts.shape
    bw = 2 * tr * C
    S, w = gemb.shape[0], gemb.shape[2]
    square_plane = F == 4
    sends = []

    def other(me, d, n):
        return lax.rem(me + d, n)

    def fsdp_to(d):
        if not square_plane:
            return lax.rem(f + d, F)
        high, low = lax.div(f, 2), lax.rem(f, 2)
        return 2 * (1 - high if d & 2 else high) + (1 - low if d & 1 else low)

    def fsdp_from(d):
        return fsdp_to(d) if square_plane else lax.rem(f + F - d, F)

    def remote(src, dst, ssem, rsem, axis, target):
        return pltpu.make_async_remote_copy(
            src_ref=src, dst_ref=dst, send_sem=ssem, recv_sem=rsem,
            device_id={axis: target}, device_id_type=pl.DeviceIdType.MESH,
        )

    def send(*args):
        copy = remote(*args)
        copy.start()
        sends.append(copy)

    def arrived(dst, ssem, rsem, axis, target):
        remote(dst, dst, ssem, rsem, axis, target).wait_recv()

    def gather_start(mine, part, size, ssem, rsem):
        for d in (1, 2) if square_plane else range(1, F):
            send(mine, part(f, 0, size), ssem(d), rsem(d), "fsdp", fsdp_to(d))

    def gather_wait(d, part, size, ssem, rsem):
        ff = fsdp_from(d)
        if not square_plane:
            arrived(part(ff, 0, size), ssem(d), rsem(d), "fsdp", ff)
        elif d < 3:
            arrived(part(ff, 0, size), ssem(d), rsem(d), "fsdp", ff)
            piece = part(ff, (d - 1) * (size // 2), size // 2)
            send(piece, piece, ssem(2 + d), rsem(2 + d), "fsdp", fsdp_to(3 - d))
        else:
            for k in (0, 1):
                arrived(part(ff, k * (size // 2), size // 2), ssem(3 + k), rsem(3 + k),
                        "fsdp", fsdp_from(2 - k))

    def share_out(block, ssem, rsem):
        for e in range(1, C):
            send(block, block, ssem(e), rsem(e), "tower", other(c, e, C))

    def shared_in(block, ssem, rsem):
        for e in range(1, C):
            cc = other(c, C - e, C)
            arrived(block(cc), ssem(e), rsem(e), "tower", cc)

    def wpart(cc):
        return lambda ff, lo, n: wall.at[pl.ds(pl.multiple_of(ff * kb + cc * kh + lo, 16), n)]

    def tpart(p, cc):
        return lambda ff, lo, n: tall.at[ff, pl.ds(pl.multiple_of((p * C + cc) * tr + lo, 16), n)]

    img_copy = pltpu.make_async_copy(images, img, loc.at[0])
    img_copy.start()
    w_copy = pltpu.make_async_copy(
        weight, wall.at[pl.ds(pl.multiple_of(f * kb, 16), kb)], loc.at[1])
    w_copy.start()
    t_copy = pltpu.make_async_copy(texts, tpart(h, c)(f, 0, tr), loc.at[2])
    t_copy.start()

    barrier = pltpu.get_barrier_semaphore()
    for axis, me, n in (("fsdp", f, F), ("tp", t, T), ("tower", c, C)):
        for d in range(1, n):
            pl.semaphore_signal(barrier, inc=1, device_id={axis: other(me, d, n)},
                                device_id_type=pl.DeviceIdType.MESH)
    pl.semaphore_wait(barrier, F + T + C - 3)

    w_sems = (lambda d: w_s.at[d]), (lambda d: w_r.at[d])
    gather_start(weight.at[pl.ds(pl.multiple_of(c * kh, 16), kh)], wpart(c), kh, *w_sems)
    partner = 2 * q + 1 - h
    send(texts, tpart(h, c)(f, 0, tr), tp_s.at[0], tp_r.at[0], "tp", partner)
    for e in range(1, C):
        send(texts, tpart(h, c)(f, 0, tr), to_s.at[0, e], to_r.at[0, e], "tower", other(c, e, C))

    img_copy.wait()
    w_copy.wait()
    aligned = kb % 128 == 0

    def by_k(ff):
        k = pl.multiple_of(ff * kb, kb)
        return jnp.dot(img[:, pl.ds(k, kb)], wall[pl.ds(k, kb), :], preferred_element_type=F32)

    if aligned:
        acc[...] = by_k(f)

    def turn(k, carry):
        k = pl.multiple_of(k * 128, 128)
        img_t[pl.ds(k, 128), :] = img[:, pl.ds(k, 128)].T
        return carry

    lax.fori_loop(0, width // 128, turn, 0)

    def wf(d):
        return (lambda e: wf_s.at[d, e]), (lambda e: wf_r.at[d, e])

    def w_from(d):
        gather_wait(d, wpart(c), kh, *w_sems)
        share_out(wpart(c)(fsdp_from(d), 0, kh), *wf(d))

    def w_rest(d):
        ff = fsdp_from(d)
        shared_in(lambda cc: wpart(cc)(ff, 0, kh), *wf(d))
        if aligned:
            acc[...] += by_k(ff)

    def t_sems(k):
        return (lambda d: t_s.at[k, d]), (lambda d: t_r.at[k, d])

    def tf(k, d):
        return (lambda e: tf_s.at[k, d, e]), (lambda e: tf_r.at[k, d, e])

    def to(k):
        return (lambda e: to_s.at[k, e]), (lambda e: to_r.at[k, e])

    sides = (h, 1 - h)
    for d in range(1, F - 1):
        w_from(d)
    gather_start(texts, tpart(h, c), tr, *t_sems(0))
    for d in range(1, F - 1):
        w_rest(d)
    theirs = tpart(1 - h, c)(f, 0, tr)
    arrived(theirs, tp_s.at[0], tp_r.at[0], "tp", partner)
    share_out(theirs, *to(1))
    w_from(F - 1)
    gather_start(theirs, tpart(1 - h, c), tr, *t_sems(1))
    w_rest(F - 1)
    if not aligned:
        acc[...] = jnp.zeros_like(acc)

        def by_tile(k, carry):
            k = pl.multiple_of(k * 128, 128)
            acc[...] += jnp.dot(img[:, pl.ds(k, 128)], wall[pl.ds(k, 128), :],
                                preferred_element_type=F32)
            return carry

        lax.fori_loop(0, width // 128, by_tile, 0)

    for k in range(2):
        eown[k] = acc[k * half : (k + 1) * half, :].astype(BF16)
    for d in range(1, T):
        tt = other(t, d, T)
        send(eown.at[lax.rem(tt, 2)], ebuf.at[t], e_s.at[d], e_r.at[d], "tp", tt)
    ebuf[t] = eown[h]

    def t_from(k, d):
        gather_wait(d, tpart(sides[k], c), tr, *t_sems(k))
        share_out(tpart(sides[k], c)(fsdp_from(d), 0, tr), *tf(k, d))

    def t_rest(k, d):
        ff = fsdp_from(d)
        shared_in(lambda cc: tpart(sides[k], cc)(ff, 0, tr), *tf(k, d))

    t_copy.wait()
    for k in range(2):
        for d in range(1, F - 1):
            t_from(k, d)
    for k in range(2):
        shared_in(lambda cc: tpart(sides[k], cc)(f, 0, tr), *to(k))

    for d in range(1, T):
        tt = other(t, T - d, T)
        arrived(ebuf.at[tt], e_s.at[d], e_r.at[d], "tp", tt)
    square = jnp.zeros((half, 1), F32)
    for k in range(T):
        part = ebuf[k].astype(F32)
        square += jnp.sum(part * part, axis=1, keepdims=True)
    rnorm = lax.rsqrt(square + epsilon)
    for k in range(T):
        ubuf[:, k * cols : (k + 1) * cols] = (ebuf[k].astype(F32) * rnorm).astype(BF16)

    span = pl.ds(pl.multiple_of(h * half, half), half)
    permf, = spread([perm[:, span].astype(F32)], 128)
    lane = lax.broadcasted_iota(jnp.int32, (1, bw), 1)

    def hits(j):
        return permf == ((j * T + 2 * q) * (bw // 2) + lane).astype(F32)

    def score(j, top):
        logit = score_scale * lax.dot_general(ubuf[...], tall[j], NT, preferred_element_type=F32)
        lbuf[j] = logit
        return jnp.maximum(top, jnp.max(logit, axis=1, keepdims=True))

    top = score(f, jnp.full((half, 1), -jnp.inf, F32))
    for d in range(1, F):
        for k in range(2):
            if d == F - 1:
                t_from(k, d)
        for k in range(2):
            t_rest(k, d)
        top = score(fsdp_from(d), top)

    def totals(j, so_far):
        total, first, positive = so_far
        logit = lbuf[j]
        power = jnp.exp(logit - top)
        return (
            total + jnp.sum(power, axis=1, keepdims=True),
            first + jnp.sum(power * logit, axis=1, keepdims=True),
            positive + jnp.sum(jnp.where(hits(j), logit, 0.0), axis=1, keepdims=True),
        )

    zero = jnp.zeros((half, 1), F32)
    total, first, positive = lax.fori_loop(0, F, totals, (zero, zero, zero))
    place = lax.broadcasted_iota(jnp.int32, (half, 128), 1)
    packed = jnp.where(place == 0, top, jnp.where(place == 1, total,
                       jnp.where(place == 2, first, jnp.where(place == 3, positive, rnorm))))
    sbuf[t] = packed.T[:8]
    for d in range(1, T):
        send(sbuf.at[t], sbuf.at[t], st_s.at[d], st_r.at[d], "tp", other(t, d, T))

    def stats_from(d):
        tt = other(t, T - d, T)
        arrived(sbuf.at[tt], st_s.at[d], st_r.at[d], "tp", tt)

    def combined(group):
        peak = sbuf[group, 0:1, :]
        for k in range(1, T // 2):
            peak = jnp.maximum(peak, sbuf[2 * k + group, 0:1, :])
        total = jnp.zeros_like(peak)
        first = jnp.zeros_like(peak)
        positive = jnp.zeros_like(peak)
        for k in range(T // 2):
            scale = jnp.exp(sbuf[2 * k + group, 0:1, :] - peak)
            total += scale * sbuf[2 * k + group, 1:2, :]
            first += scale * sbuf[2 * k + group, 2:3, :]
            positive += sbuf[2 * k + group, 3:4, :]
        return peak + jnp.log(total), first / total, positive

    def sign_of(places):
        return 1.0 - 2.0 * forget[:, places].astype(F32)

    for d in range(2, T, 2):
        stats_from(d)
    lse_row, _, _ = combined(h)
    lse, sign = spread([lse_row, sign_of(span)], 128)

    def weigh(j, carry):
        pbuf[j] = (sign * (jnp.exp(lbuf[j] - lse) - hits(j).astype(F32))).astype(BF16)
        return carry

    lax.fori_loop(0, F, weigh, 0)

    def grad_for(tt):
        place = pl.ds(pl.multiple_of(tt * cols, cols), cols)
        total = jnp.dot(pbuf[0], tall[0, :, place], preferred_element_type=F32)
        for j in range(1, F):
            total += jnp.dot(pbuf[j], tall[j, :, place], preferred_element_type=F32)
        return score_scale * total

    for d in range(1, T):
        tt = other(t, d, T)
        partial = grad_for(tt).astype(BF16)
        for s in range(S):
            gsend[d, s] = partial[:, s * w : (s + 1) * w]
        send(gsend.at[d, 0], grecv.at[t, 0], g_s.at[d, 0], g_r.at[d, 0], "tp", tt)
    for s in range(1, S):
        for d in range(1, T):
            send(gsend.at[d, s], grecv.at[t, s], g_s.at[d, s], g_r.at[d, s], "tp", other(t, d, T))
    gown[h] = grad_for(t)
    gown[1 - h] = jnp.zeros((half, cols), F32)
    grecv[t] = jnp.zeros((S, half, w), BF16)

    for d in range(1, T, 2):
        stats_from(d)
    kept = []
    for k in range(2):
        places = slice(k * half, (k + 1) * half)
        lse_row, mean_row, positive = combined(k)
        loss[:, places] = lse_row - positive
        kept.append(spread([sign_of(places) * (mean_row - positive), sbuf[k, 4:5, :]], 128))

    def block(s, ff, cc):
        k = pl.multiple_of(ff * kb + cc * kh, 16)
        return jnp.dot(img_t[pl.ds(k, kh), :], gemb[s], preferred_element_type=F32)

    def compute(s, d):
        ff = fsdp_to(d)
        for e in range(1, C):
            cc = other(c, e, C)
            sib_send[s, d, e] = block(s, ff, cc)
            send(sib_send.at[s, d, e], sib_recv.at[s, d, e], b_s.at[s, d, e], b_r.at[s, d, e],
                 "tower", cc)
        share[s, d] = block(s, ff, c)

    def join(s, d):
        total = share[s, d]
        for e in range(1, C):
            arrived(sib_recv.at[s, d, e], b_s.at[s, d, e], b_r.at[s, d, e],
                    "tower", other(c, C - e, C))
            total += sib_recv[s, d, e]
        share[s, d] = total

    hh = kh // 2

    def put(s, slot, value, target):
        wsend[s, slot] = value.astype(BF16)
        send(wsend.at[s, slot], wrecv.at[s, slot], x_s.at[s, slot], x_r.at[s, slot], "fsdp", target)

    def got(s, slot, source):
        arrived(wrecv.at[s, slot], x_s.at[s, slot], x_r.at[s, slot], "fsdp", source)
        return wrecv[s, slot].astype(F32)

    def scatter(s):
        for d in range(1, T):
            tt = other(t, T - d, T)
            arrived(grecv.at[tt, s], g_s.at[d, s], g_r.at[d, s], "tp", tt)
        places = slice(s * w, (s + 1) * w)
        for k in range(2):
            radial, rnorm = kept[k]
            grad = gown[k, :, places]
            for j in range(T // 2):
                grad += grecv[2 * j + k, s].astype(F32)
            unit = eown[k, :, places].astype(F32) * rnorm
            gemb[s, k * half : (k + 1) * half, :] = (rnorm * (grad - unit * radial)).astype(BF16)
        if not square_plane:
            for d in range(F - 1, 0, -1):
                compute(s, d)
                if d < F - 1:
                    join(s, d + 1)
                    for k in range(2):
                        put(s, 2 * (d + 1) + k, share[s, d + 1, k * hh : (k + 1) * hh], fsdp_to(d + 1))
            compute(s, 0)
            join(s, 1)
            for k in range(2):
                put(s, 2 + k, share[s, 1, k * hh : (k + 1) * hh], fsdp_to(1))
            return
        compute(s, 3)
        compute(s, 1)
        join(s, 3)
        put(s, 6, share[s, 3, :hh], fsdp_to(1))
        put(s, 7, share[s, 3, hh:], fsdp_to(2))
        compute(s, 2)
        join(s, 1)
        put(s, 2, share[s, 1, :hh], fsdp_to(1))
        compute(s, 0)
        join(s, 2)
        put(s, 5, share[s, 2, hh:], fsdp_to(2))
        put(s, 3, share[s, 1, hh:] + got(s, 7, fsdp_from(2)), fsdp_to(1))
        put(s, 4, share[s, 2, :hh] + got(s, 6, fsdp_from(1)), fsdp_to(2))

    def o_sems(s):
        return (lambda e: o_s.at[s, e]), (lambda e: o_r.at[s, e])

    def home(s, cc, k):
        copy = pltpu.make_async_copy(
            obuf.at[s, cc], out.at[cc, :, pl.ds(s * w, w)], loc.at[3 + s * C + k])
        copy.start()
        return copy

    for s in range(S):
        scatter(s)
    homes = []
    for s in range(S):
        join(s, 0)
        for k in range(2):
            total = share[s, 0, k * hh : (k + 1) * hh]
            for d in range(1, 3 if square_plane else F):
                total += got(s, 2 * d + k, fsdp_from(d))
            obuf[s, c, k * hh : (k + 1) * hh, :] = total
        share_out(obuf.at[s, c], *o_sems(s))
        homes.append(home(s, c, 0))
    for s in range(S):
        for e in range(1, C):
            cc = other(c, C - e, C)
            arrived(obuf.at[s, cc], o_s.at[s, e], o_r.at[s, e], "tower", cc)
            homes.append(home(s, cc, e))
    for copy in homes:
        copy.wait()
    for copy in sends:
        copy.wait_send()


def local(images, weight, texts, perm, forget):
    F, T, C = lax.axis_size("fsdp"), lax.axis_size("tp"), lax.axis_size("tower")
    assert T % 2 == 0
    pairs, width = images.shape
    kb, cols = weight.shape
    kh = kb // C
    tr, embed = texts.shape
    half = pairs // 2
    bw = 2 * tr * C
    S = 2 if cols % 256 == 0 else 1
    w = cols // S
    vmem, dma = pltpu.VMEM, pltpu.SemaphoreType.DMA
    scratch = [
        vmem((pairs, width), BF16),
        vmem((width, pairs), BF16),
        vmem((width, cols), BF16),
        vmem((F, bw, embed), BF16),
        vmem((pairs, cols), F32),
        vmem((2, half, cols), BF16),
        vmem((T, half, cols), BF16),
        vmem((half, embed), BF16),
        vmem((F, half, bw), F32),
        vmem((F, half, bw), BF16),
        vmem((T, 8, half), F32),
        vmem((2, half, cols), F32),
        vmem((T, S, half, w), BF16),
        vmem((T, S, half, w), BF16),
        vmem((S, pairs, w), BF16),
        vmem((S, F, kh, w), F32),
        vmem((S, F, C, kh, w), F32),
        vmem((S, F, C, kh, w), F32),
        vmem((S, 2 * F, kh // 2, w), BF16),
        vmem((S, 2 * F, kh // 2, w), BF16),
        vmem((S, C, kh, w), F32),
        dma((3 + S * C,)),
        dma((F + 1,)), dma((F + 1,)), dma((F, C)), dma((F, C)),
        dma((2, F + 1)), dma((2, F + 1)), dma((2, F, C)), dma((2, F, C)),
        dma((2, C)), dma((2, C)), dma((1,)), dma((1,)),
        dma((T,)), dma((T,)), dma((T,)), dma((T,)),
        dma((T, S)), dma((T, S)),
        dma((S, F, C)), dma((S, F, C)), dma((S, 2 * F)), dma((S, 2 * F)),
        dma((S, C)), dma((S, C)),
    ]
    any_space = pl.BlockSpec(memory_space=pl.ANY)
    whole = pl.BlockSpec(memory_space=pltpu.VMEM)
    loss, out = pl.pallas_call(
        functools.partial(kernel, (F, T, C)),
        out_shape=(
            jax.ShapeDtypeStruct((1, pairs), F32),
            jax.ShapeDtypeStruct((C, kh, cols), F32),
        ),
        in_specs=[any_space, any_space, any_space, whole, whole],
        out_specs=(whole, any_space),
        scratch_shapes=scratch,
        compiler_params=pltpu.CompilerParams(
            collective_id=0, has_side_effects=True, vmem_limit_bytes=60 * 2**20
        ),
        cost_estimate=pl.CostEstimate(
            flops=4 * pairs * cols * width + 4 * half * F * bw * embed,
            bytes_accessed=2 * (pairs * width + kb * cols + tr * embed) + 4 * kb * cols,
            transcendentals=2 * half * F * bw,
        ),
    )(images, weight, texts, perm.reshape(1, pairs), forget.reshape(1, pairs))
    return loss.reshape(pairs), out.reshape(kb, cols)


def solution(mesh):
    return jax.shard_map(
        local,
        mesh=mesh,
        in_specs=(
            P(("fsdp", "tower"), None),
            P("fsdp", "tp"),
            P(("fsdp", "tp", "tower"), None),
            P(("fsdp", "tower")),
            P(("fsdp", "tower")),
        ),
        out_specs=(P(("fsdp", "tower")), P("fsdp", "tp")),
        check_vma=False,
    )
```

```python
import functools

import jax
import jax.numpy as jnp
from jax import lax
from jax.experimental import pallas as pl
from jax.experimental.pallas import tpu as pltpu
from jax.sharding import PartitionSpec as P

epsilon = 1e-06
score_scale = 100.0
F32 = jnp.float32
BF16 = jnp.bfloat16
NT = (((1,), (1,)), ((), ()))


def spread(columns, lanes):
    n = columns[0].shape[1]
    which = lax.broadcasted_iota(jnp.int32, (lanes, n), 0)
    block = jnp.broadcast_to(columns[0], (lanes, n))
    for k in range(1, len(columns)):
        block = jnp.where(which == k, columns[k], block)
    block = block.T
    return [block[:, k : k + 1] for k in range(len(columns))]


def kernel(sizes, images, weight, texts, perm, forget, loss, out, *scratch):
    F, T, C = sizes
    (img, img_t, wall, tall, acc, eown, ebuf, ubuf, lbuf, pbuf, sbuf, gown, gsend, grecv, gemb,
     share, sib_send, sib_recv, wsend, wrecv, obuf,
     loc, w_s, w_r, wf_s, wf_r, t_s, t_r, tf_s, tf_r, to_s, to_r, tp_s, tp_r, e_s, e_r, st_s, st_r,
     g_s, g_r, b_s, b_r, x_s, x_r, o_s, o_r) = scratch
    f, t, c = lax.axis_index("fsdp"), lax.axis_index("tp"), lax.axis_index("tower")
    q, h = lax.div(t, 2), lax.rem(t, 2)
    pairs, width = img.shape
    half = pairs // 2
    kb, cols = weight.shape
    kh = kb // C
    tr, embed = texts.shape
    bw = 2 * tr * C
    S, w = gemb.shape[0], gemb.shape[2]
    square_plane = F == 4
    sends = []

    def other(me, d, n):
        return lax.rem(me + d, n)

    def fsdp_to(d):
        if not square_plane:
            return lax.rem(f + d, F)
        high, low = lax.div(f, 2), lax.rem(f, 2)
        return 2 * (1 - high if d & 2 else high) + (1 - low if d & 1 else low)

    def fsdp_from(d):
        return fsdp_to(d) if square_plane else lax.rem(f + F - d, F)

    def remote(src, dst, ssem, rsem, axis, target):
        return pltpu.make_async_remote_copy(
            src_ref=src, dst_ref=dst, send_sem=ssem, recv_sem=rsem,
            device_id={axis: target}, device_id_type=pl.DeviceIdType.MESH,
        )

    def send(*args):
        copy = remote(*args)
        copy.start()
        sends.append(copy)

    def arrived(dst, ssem, rsem, axis, target):
        remote(dst, dst, ssem, rsem, axis, target).wait_recv()

    def gather_start(mine, part, size, ssem, rsem):
        for d in (1, 2) if square_plane else range(1, F):
            send(mine, part(f, 0, size), ssem(d), rsem(d), "fsdp", fsdp_to(d))

    def gather_wait(d, part, size, ssem, rsem):
        ff = fsdp_from(d)
        if not square_plane:
            arrived(part(ff, 0, size), ssem(d), rsem(d), "fsdp", ff)
        elif d < 3:
            arrived(part(ff, 0, size), ssem(d), rsem(d), "fsdp", ff)
            piece = part(ff, (d - 1) * (size // 2), size // 2)
            send(piece, piece, ssem(2 + d), rsem(2 + d), "fsdp", fsdp_to(3 - d))
        else:
            for k in (0, 1):
                arrived(part(ff, k * (size // 2), size // 2), ssem(3 + k), rsem(3 + k),
                        "fsdp", fsdp_from(2 - k))

    def share_out(block, ssem, rsem):
        for e in range(1, C):
            send(block, block, ssem(e), rsem(e), "tower", other(c, e, C))

    def shared_in(block, ssem, rsem):
        for e in range(1, C):
            cc = other(c, C - e, C)
            arrived(block(cc), ssem(e), rsem(e), "tower", cc)

    def wpart(cc):
        return lambda ff, lo, n: wall.at[pl.ds(pl.multiple_of(ff * kb + cc * kh + lo, 16), n)]

    def tpart(p, cc):
        return lambda ff, lo, n: tall.at[ff, pl.ds(pl.multiple_of((p * C + cc) * tr + lo, 16), n)]

    img_copy = pltpu.make_async_copy(images, img, loc.at[0])
    img_copy.start()
    w_copy = pltpu.make_async_copy(
        weight, wall.at[pl.ds(pl.multiple_of(f * kb, 16), kb)], loc.at[1])
    w_copy.start()
    t_copy = pltpu.make_async_copy(texts, tpart(h, c)(f, 0, tr), loc.at[2])
    t_copy.start()

    barrier = pltpu.get_barrier_semaphore()
    for axis, me, n in (("fsdp", f, F), ("tp", t, T), ("tower", c, C)):
        for d in range(1, n):
            pl.semaphore_signal(barrier, inc=1, device_id={axis: other(me, d, n)},
                                device_id_type=pl.DeviceIdType.MESH)
    pl.semaphore_wait(barrier, F + T + C - 3)

    w_sems = (lambda d: w_s.at[d]), (lambda d: w_r.at[d])
    gather_start(weight.at[pl.ds(pl.multiple_of(c * kh, 16), kh)], wpart(c), kh, *w_sems)
    partner = 2 * q + 1 - h
    send(texts, tpart(h, c)(f, 0, tr), tp_s.at[0], tp_r.at[0], "tp", partner)
    for e in range(1, C):
        send(texts, tpart(h, c)(f, 0, tr), to_s.at[0, e], to_r.at[0, e], "tower", other(c, e, C))

    img_copy.wait()
    w_copy.wait()
    aligned = kb % 128 == 0

    def by_k(ff):
        k = pl.multiple_of(ff * kb, kb)
        return jnp.dot(img[:, pl.ds(k, kb)], wall[pl.ds(k, kb), :], preferred_element_type=F32)

    if aligned:
        acc[...] = by_k(f)

    def turn(k, carry):
        k = pl.multiple_of(k * 128, 128)
        img_t[pl.ds(k, 128), :] = img[:, pl.ds(k, 128)].T
        return carry

    early = width // 256
    lax.fori_loop(0, early, turn, 0)

    def wf(d):
        return (lambda e: wf_s.at[d, e]), (lambda e: wf_r.at[d, e])

    def w_from(d):
        gather_wait(d, wpart(c), kh, *w_sems)
        share_out(wpart(c)(fsdp_from(d), 0, kh), *wf(d))

    def w_rest(d):
        ff = fsdp_from(d)
        shared_in(lambda cc: wpart(cc)(ff, 0, kh), *wf(d))
        if aligned:
            acc[...] += by_k(ff)

    def t_sems(k):
        return (lambda d: t_s.at[k, d]), (lambda d: t_r.at[k, d])

    def tf(k, d):
        return (lambda e: tf_s.at[k, d, e]), (lambda e: tf_r.at[k, d, e])

    def to(k):
        return (lambda e: to_s.at[k, e]), (lambda e: to_r.at[k, e])

    sides = (h, 1 - h)
    for d in range(1, F - 1):
        w_from(d)
    gather_start(texts, tpart(h, c), tr, *t_sems(0))
    for d in range(1, F - 1):
        w_rest(d)
    theirs = tpart(1 - h, c)(f, 0, tr)
    arrived(theirs, tp_s.at[0], tp_r.at[0], "tp", partner)
    share_out(theirs, *to(1))
    w_from(F - 1)
    gather_start(theirs, tpart(1 - h, c), tr, *t_sems(1))
    w_rest(F - 1)
    if not aligned:
        acc[...] = jnp.zeros_like(acc)

        def by_tile(k, carry):
            k = pl.multiple_of(k * 128, 128)
            acc[...] += jnp.dot(img[:, pl.ds(k, 128)], wall[pl.ds(k, 128), :],
                                preferred_element_type=F32)
            return carry

        lax.fori_loop(0, width // 128, by_tile, 0)

    for k in range(2):
        eown[k] = acc[k * half : (k + 1) * half, :].astype(BF16)
    for d in range(1, T):
        tt = other(t, d, T)
        send(eown.at[lax.rem(tt, 2)], ebuf.at[t], e_s.at[d], e_r.at[d], "tp", tt)
    ebuf[t] = eown[h]

    def t_from(k, d):
        gather_wait(d, tpart(sides[k], c), tr, *t_sems(k))
        share_out(tpart(sides[k], c)(fsdp_from(d), 0, tr), *tf(k, d))

    def t_rest(k, d):
        ff = fsdp_from(d)
        shared_in(lambda cc: tpart(sides[k], cc)(ff, 0, tr), *tf(k, d))

    t_copy.wait()
    for k in range(2):
        for d in range(1, F - 1):
            t_from(k, d)
    for k in range(2):
        shared_in(lambda cc: tpart(sides[k], cc)(f, 0, tr), *to(k))

    for d in range(1, T):
        tt = other(t, T - d, T)
        arrived(ebuf.at[tt], e_s.at[d], e_r.at[d], "tp", tt)
    square = jnp.zeros((half, 1), F32)
    for k in range(T):
        part = ebuf[k].astype(F32)
        square += jnp.sum(part * part, axis=1, keepdims=True)
    rnorm = lax.rsqrt(square + epsilon)
    for k in range(T):
        ubuf[:, k * cols : (k + 1) * cols] = (ebuf[k].astype(F32) * rnorm).astype(BF16)

    span = pl.ds(pl.multiple_of(h * half, half), half)
    permf, = spread([perm[:, span].astype(F32)], 128)
    lane = lax.broadcasted_iota(jnp.int32, (1, bw), 1)

    def hits(j):
        return permf == ((j * T + 2 * q) * (bw // 2) + lane).astype(F32)

    def score(j, so_far):
        top, total, first, positive = so_far
        lbuf[j] = score_scale * lax.dot_general(
            ubuf[...], tall[j], NT, preferred_element_type=F32)
        logit = lbuf[j]
        peak = jnp.maximum(top, jnp.max(logit, axis=1, keepdims=True))
        scale = jnp.exp(top - peak)
        power = jnp.exp(logit - peak)
        return (
            peak,
            total * scale + jnp.sum(power, axis=1, keepdims=True),
            first * scale + jnp.sum(power * logit, axis=1, keepdims=True),
            positive + jnp.sum(jnp.where(hits(j), logit, 0.0), axis=1, keepdims=True),
        )

    zero = jnp.zeros((half, 1), F32)
    so_far = score(f, (jnp.full((half, 1), -jnp.inf, F32), zero, zero, zero))
    for d in range(1, F):
        if d == F - 1:
            for k in range(2):
                t_from(k, d)
        for k in range(2):
            t_rest(k, d)
        so_far = score(fsdp_from(d), so_far)
    top, total, first, positive = so_far
    place = lax.broadcasted_iota(jnp.int32, (half, 128), 1)
    packed = jnp.where(place == 0, top, jnp.where(place == 1, total,
                       jnp.where(place == 2, first, jnp.where(place == 3, positive, rnorm))))
    sbuf[t] = packed.T[:8]
    for d in (*range(2, T, 2), *range(1, T, 2)):
        send(sbuf.at[t], sbuf.at[t], st_s.at[d], st_r.at[d], "tp", other(t, d, T))

    lax.fori_loop(early, width // 128, turn, 0)

    def stats_from(d):
        tt = other(t, T - d, T)
        arrived(sbuf.at[tt], st_s.at[d], st_r.at[d], "tp", tt)

    def combined(group):
        peak = sbuf[group, 0:1, :]
        for k in range(1, T // 2):
            peak = jnp.maximum(peak, sbuf[2 * k + group, 0:1, :])
        total = jnp.zeros_like(peak)
        first = jnp.zeros_like(peak)
        positive = jnp.zeros_like(peak)
        for k in range(T // 2):
            scale = jnp.exp(sbuf[2 * k + group, 0:1, :] - peak)
            total += scale * sbuf[2 * k + group, 1:2, :]
            first += scale * sbuf[2 * k + group, 2:3, :]
            positive += sbuf[2 * k + group, 3:4, :]
        return peak + jnp.log(total), first / total, positive

    def sign_of(places):
        return 1.0 - 2.0 * forget[:, places].astype(F32)

    for d in range(2, T, 2):
        stats_from(d)
    lse_row, _, _ = combined(h)
    lse, sign = spread([lse_row, sign_of(span)], 128)

    def weigh(j, carry):
        pbuf[j] = (sign * (jnp.exp(lbuf[j] - lse) - hits(j).astype(F32))).astype(BF16)
        return carry

    lax.fori_loop(0, F, weigh, 0)

    def grad_for(tt):
        place = pl.ds(pl.multiple_of(tt * cols, cols), cols)
        total = jnp.dot(pbuf[0], tall[0, :, place], preferred_element_type=F32)
        for j in range(1, F):
            total += jnp.dot(pbuf[j], tall[j, :, place], preferred_element_type=F32)
        return score_scale * total

    for d in range(1, T):
        tt = other(t, d, T)
        partial = grad_for(tt).astype(BF16)
        for s in range(S):
            gsend[d, s] = partial[:, s * w : (s + 1) * w]
        send(gsend.at[d, 0], grecv.at[t, 0], g_s.at[d, 0], g_r.at[d, 0], "tp", tt)
    for s in range(1, S):
        for d in range(1, T):
            send(gsend.at[d, s], grecv.at[t, s], g_s.at[d, s], g_r.at[d, s], "tp", other(t, d, T))
    gown[h] = grad_for(t)
    gown[1 - h] = jnp.zeros((half, cols), F32)
    grecv[t] = jnp.zeros((S, half, w), BF16)

    for d in range(1, T, 2):
        stats_from(d)
    kept = []
    for k in range(2):
        places = slice(k * half, (k + 1) * half)
        lse_row, mean_row, positive = combined(k)
        loss[:, places] = lse_row - positive
        kept.append(spread([sign_of(places) * (mean_row - positive), sbuf[k, 4:5, :]], 128))

    def block(s, ff, cc):
        k = pl.multiple_of(ff * kb + cc * kh, 16)
        return jnp.dot(img_t[pl.ds(k, kh), :], gemb[s], preferred_element_type=F32)

    def compute(s, d):
        ff = fsdp_to(d)
        for e in range(1, C):
            cc = other(c, e, C)
            sib_send[s, d, e] = block(s, ff, cc)
            send(sib_send.at[s, d, e], sib_recv.at[s, d, e], b_s.at[s, d, e], b_r.at[s, d, e],
                 "tower", cc)
        share[s, d] = block(s, ff, c)

    def join(s, d):
        total = share[s, d]
        for e in range(1, C):
            arrived(sib_recv.at[s, d, e], b_s.at[s, d, e], b_r.at[s, d, e],
                    "tower", other(c, C - e, C))
            total += sib_recv[s, d, e]
        share[s, d] = total

    hh = kh // 2

    def put(s, slot, value, target):
        wsend[s, slot] = value.astype(BF16)
        send(wsend.at[s, slot], wrecv.at[s, slot], x_s.at[s, slot], x_r.at[s, slot], "fsdp", target)

    def got(s, slot, source):
        arrived(wrecv.at[s, slot], x_s.at[s, slot], x_r.at[s, slot], "fsdp", source)
        return wrecv[s, slot].astype(F32)

    def scatter(s):
        for d in range(1, T):
            tt = other(t, T - d, T)
            arrived(grecv.at[tt, s], g_s.at[d, s], g_r.at[d, s], "tp", tt)
        places = slice(s * w, (s + 1) * w)
        for k in range(2):
            radial, rnorm = kept[k]
            grad = gown[k, :, places]
            for j in range(T // 2):
                grad += grecv[2 * j + k, s].astype(F32)
            unit = eown[k, :, places].astype(F32) * rnorm
            gemb[s, k * half : (k + 1) * half, :] = (rnorm * (grad - unit * radial)).astype(BF16)
        if not square_plane:
            for d in range(F - 1, 0, -1):
                compute(s, d)
                if d < F - 1:
                    join(s, d + 1)
                    for k in range(2):
                        put(s, 2 * (d + 1) + k, share[s, d + 1, k * hh : (k + 1) * hh], fsdp_to(d + 1))
            compute(s, 0)
            join(s, 1)
            for k in range(2):
                put(s, 2 + k, share[s, 1, k * hh : (k + 1) * hh], fsdp_to(1))
            return
        compute(s, 3)
        compute(s, 1)
        join(s, 3)
        put(s, 6, share[s, 3, :hh], fsdp_to(1))
        put(s, 7, share[s, 3, hh:], fsdp_to(2))
        compute(s, 2)
        join(s, 1)
        put(s, 2, share[s, 1, :hh], fsdp_to(1))
        compute(s, 0)
        join(s, 2)
        put(s, 5, share[s, 2, hh:], fsdp_to(2))
        put(s, 3, share[s, 1, hh:] + got(s, 7, fsdp_from(2)), fsdp_to(1))
        put(s, 4, share[s, 2, :hh] + got(s, 6, fsdp_from(1)), fsdp_to(2))

    def o_sems(s):
        return (lambda e: o_s.at[s, e]), (lambda e: o_r.at[s, e])

    def home(s, cc, k):
        copy = pltpu.make_async_copy(
            obuf.at[s, cc], out.at[cc, :, pl.ds(s * w, w)], loc.at[3 + s * C + k])
        copy.start()
        return copy

    for s in range(S):
        scatter(s)
    homes = []
    for s in range(S):
        join(s, 0)
        for k in range(2):
            total = share[s, 0, k * hh : (k + 1) * hh]
            for d in range(1, 3 if square_plane else F):
                total += got(s, 2 * d + k, fsdp_from(d))
            obuf[s, c, k * hh : (k + 1) * hh, :] = total
        share_out(obuf.at[s, c], *o_sems(s))
        homes.append(home(s, c, 0))
    for s in range(S):
        for e in range(1, C):
            cc = other(c, C - e, C)
            arrived(obuf.at[s, cc], o_s.at[s, e], o_r.at[s, e], "tower", cc)
            homes.append(home(s, cc, e))
    for copy in homes:
        copy.wait()
    for copy in sends:
        copy.wait_send()


def local(images, weight, texts, perm, forget):
    F, T, C = lax.axis_size("fsdp"), lax.axis_size("tp"), lax.axis_size("tower")
    assert T % 2 == 0
    pairs, width = images.shape
    kb, cols = weight.shape
    kh = kb // C
    tr, embed = texts.shape
    half = pairs // 2
    bw = 2 * tr * C
    S = 2 if cols % 256 == 0 else 1
    w = cols // S
    vmem, dma = pltpu.VMEM, pltpu.SemaphoreType.DMA
    scratch = [
        vmem((pairs, width), BF16),
        vmem((width, pairs), BF16),
        vmem((width, cols), BF16),
        vmem((F, bw, embed), BF16),
        vmem((pairs, cols), F32),
        vmem((2, half, cols), BF16),
        vmem((T, half, cols), BF16),
        vmem((half, embed), BF16),
        vmem((F, half, bw), F32),
        vmem((F, half, bw), BF16),
        vmem((T, 8, half), F32),
        vmem((2, half, cols), F32),
        vmem((T, S, half, w), BF16),
        vmem((T, S, half, w), BF16),
        vmem((S, pairs, w), BF16),
        vmem((S, F, kh, w), F32),
        vmem((S, F, C, kh, w), F32),
        vmem((S, F, C, kh, w), F32),
        vmem((S, 2 * F, kh // 2, w), BF16),
        vmem((S, 2 * F, kh // 2, w), BF16),
        vmem((S, C, kh, w), F32),
        dma((3 + S * C,)),
        dma((F + 1,)), dma((F + 1,)), dma((F, C)), dma((F, C)),
        dma((2, F + 1)), dma((2, F + 1)), dma((2, F, C)), dma((2, F, C)),
        dma((2, C)), dma((2, C)), dma((1,)), dma((1,)),
        dma((T,)), dma((T,)), dma((T,)), dma((T,)),
        dma((T, S)), dma((T, S)),
        dma((S, F, C)), dma((S, F, C)), dma((S, 2 * F)), dma((S, 2 * F)),
        dma((S, C)), dma((S, C)),
    ]
    any_space = pl.BlockSpec(memory_space=pl.ANY)
    whole = pl.BlockSpec(memory_space=pltpu.VMEM)
    loss, out = pl.pallas_call(
        functools.partial(kernel, (F, T, C)),
        out_shape=(
            jax.ShapeDtypeStruct((1, pairs), F32),
            jax.ShapeDtypeStruct((C, kh, cols), F32),
        ),
        in_specs=[any_space, any_space, any_space, whole, whole],
        out_specs=(whole, any_space),
        scratch_shapes=scratch,
        compiler_params=pltpu.CompilerParams(
            collective_id=0, has_side_effects=True, vmem_limit_bytes=60 * 2**20
        ),
        cost_estimate=pl.CostEstimate(
            flops=4 * pairs * cols * width + 4 * half * F * bw * embed,
            bytes_accessed=2 * (pairs * width + kb * cols + tr * embed) + 4 * kb * cols,
            transcendentals=2 * half * F * bw,
        ),
    )(images, weight, texts, perm.reshape(1, pairs), forget.reshape(1, pairs))
    return loss.reshape(pairs), out.reshape(kb, cols)


def solution(mesh):
    return jax.shard_map(
        local,
        mesh=mesh,
        in_specs=(
            P(("fsdp", "tower"), None),
            P("fsdp", "tp"),
            P(("fsdp", "tp", "tower"), None),
            P(("fsdp", "tower")),
            P(("fsdp", "tower")),
        ),
        out_specs=(P(("fsdp", "tower")), P("fsdp", "tp")),
        check_vma=False,
    )
```
